256 devices in a mesh: dp: 32 (over z, y), frame: 8 (over x, core).
Axes of the slice: x: 4, y: 4, z: 8, core: 2. Of those that a mesh axis runs over, the one named last changes fastest.
Arguments:
- qkv: bfloat16 [32, 8, 192, 4224], P('dp', 'frame'), may hold values from -24 to 24
- keep: int32 [32, 8, 192], P('dp', 'frame'), may hold values from 0 to 255, as said below
- counts: int32 [32, 8], P('dp', 'frame'), may hold values from 96 to 192, as said below
- grad_out: bfloat16 [32, 8, 192, 1408], P('dp', 'frame'), may hold values from -6 to 6
- w_out: bfloat16 [1408, 1408], P('dp', 'frame'), may hold values from -0.15625 to 0.15625
Outputs:
- mixed: bfloat16 [32, 8, 192, 1408], P('dp', 'frame')
- grad_qkv: bfloat16 [32, 8, 192, 4224], P('dp', 'frame')
- grad_w_out: float32 [1408, 1408], P('dp', 'frame')
The draws below stay inside these ranges and needn't reach their ends.
Inputs may be any that keep to these rules, and one draw needn't show every extreme that they name: `keep`: the 192 entries of one frame are distinct and increasing; slots past the frame's count hold positions too, which are not used. `counts`: every clip has a frame whose 192 slots are all valid.
All inputs are finite; a program needn't handle non-finite values.
Results may differ from the reference program's by a relative error of at most 0.0057.
Values may be sent and summed in bfloat16 or wider, within the bound.
No kernel may reach another device: no remote copies, remote signals or barrier semaphores. Data moves between devices by JAX's collectives and lax.ppermute only.
A program may use at most 128 MiB of HBM per device.

```python
import math
import jax
import jax.numpy as jnp
from jax import lax

D = 1408
HEADS = 16
PATCHES = 256
CAP = 192
FRAMES = 8
CLIPS = 32


def draw_qkv(key, part):
    key = jax.random.fold_in(key, 11)
    key_base = jax.random.fold_in(key, 0)
    shape_all = (CLIPS, FRAMES, CAP, 3 * D)
    base = jax.random.normal(key_base, shape_all, jnp.float32)
    full = base
    return jnp.clip(full, -24.0, 24.0).astype(jnp.bfloat16)


def draw_keep(key, part):
    key = jax.random.fold_in(key, 23)
    frame_keys = jax.random.split(key, CLIPS * FRAMES)

    def pick_frame(frame_key):
        return jax.random.permutation(frame_key, PATCHES)[:CAP]
    chosen = jax.vmap(pick_frame)(frame_keys)
    return jnp.sort(chosen, axis=-1).reshape(CLIPS, FRAMES, CAP).astype(jnp.int32)


def draw_counts(key, part):
    key = jax.random.fold_in(key, 37)
    key_drawn, key_full = jax.random.split(key)
    drawn = jax.random.randint(key_drawn, (CLIPS, FRAMES), CAP // 2, CAP + 1, jnp.int32)
    full_frame = jax.random.randint(key_full, (CLIPS, 1), 0, FRAMES, jnp.int32)
    frame_index = jnp.arange(FRAMES, dtype=jnp.int32)[None, :]
    return jnp.where(frame_index == full_frame, CAP, drawn).astype(jnp.int32)


def block_scale(own_key, extent, cuts, least, high):
    gain, own = 1.0, jax.random.fold_in(own_key, 6)
    for dim, parts in cuts:
        draws = jnp.exp(jax.random.uniform(jax.random.fold_in(own, dim), (parts,), jnp.float32, least / len(cuts), high / len(cuts)))
        gain = gain * jnp.repeat(draws, extent[dim] // parts).reshape([-1 if axis == dim else 1 for axis in range(len(extent))])
    return gain


def noise(key, shape, width, most, cuts=(), kind=jnp.bfloat16):
    loudness = block_scale(key, shape, cuts, -0.22, 0.18) if cuts else 1.0
    values = jax.random.normal(key, shape, jnp.float32) * width * loudness
    return jnp.minimum(jnp.maximum(values, -most), most).astype(kind)


def setup_inputs(seed: int = 0) -> dict:
    key_of = jax.random.split(jax.random.key(seed), 6)
    qkv = draw_qkv(jax.random.fold_in(key_of[5], 71), 0)
    keep = draw_keep(jax.random.fold_in(key_of[5], 71), 0)
    counts = draw_counts(jax.random.fold_in(key_of[5], 71), 0)
    grad_out = noise(key_of[3], (CLIPS, FRAMES, CAP, D), 1.0, 6.0, ((0, 32), (1, 8)))
    w_out = noise(key_of[4], (D, D), D ** -0.5, 0.15625, ((0, 32), (1, 8)))
    return dict(qkv=qkv, keep=keep, counts=counts, grad_out=grad_out, w_out=w_out)


def attention_forward(grid, kept):
    frames_all, patches_all, triple = grid.shape
    width_all = triple // 3
    head_size = width_all // HEADS
    shape_heads = (frames_all, patches_all, HEADS, head_size)
    query_part = grid[..., :width_all].reshape(shape_heads).astype(jnp.float32)
    key_part = grid[..., width_all:2 * width_all].reshape(shape_heads).astype(jnp.float32)
    value_part = grid[..., 2 * width_all:].reshape(shape_heads).astype(jnp.float32)
    scaling = 1.0 / math.sqrt(head_size)
    scores = jnp.einsum('tphd,sphd->phts', query_part, key_part) * scaling
    present = (jnp.transpose(kept) > 0)[:, None, None, :]
    scores = jnp.where(present, scores, -1e+30)
    expo = jnp.exp(scores - lax.optimization_barrier(jnp.max(scores, axis=-1, keepdims=True)))
    soft_full = expo / lax.optimization_barrier(jnp.sum(expo, axis=-1, keepdims=True))
    soft_half = soft_full.astype(jnp.bfloat16)
    heads_out = jnp.einsum('phts,sphd->tphd', soft_half.astype(jnp.float32), value_part)
    att_grid = heads_out.astype(jnp.bfloat16).reshape(frames_all, patches_all, width_all)
    return (att_grid, (query_part, key_part, value_part, soft_full, soft_half))

def attention_backward(saved, grad_grid):
    query_part, key_part, value_part, soft_full, soft_half = saved
    frames_all, patches_all, heads_all, head_size = query_part.shape
    scaling = 1.0 / math.sqrt(head_size)
    grad_heads = grad_grid.reshape(query_part.shape).astype(jnp.float32)
    grad_soft = jnp.einsum('tphd,sphd->phts', grad_heads, value_part)
    grad_value = jnp.einsum('phts,tphd->sphd', soft_half.astype(jnp.float32), grad_heads).astype(jnp.bfloat16)
    inner = lax.optimization_barrier(jnp.sum(soft_full * grad_soft, axis=-1, keepdims=True))
    grad_score = (soft_full * (grad_soft - inner)).astype(jnp.bfloat16).astype(jnp.float32)
    grad_query = (jnp.einsum('phts,sphd->tphd', grad_score, key_part) * scaling).astype(jnp.bfloat16)
    grad_key = (jnp.einsum('phts,tphd->sphd', grad_score, query_part) * scaling).astype(jnp.bfloat16)
    flat_shape = (frames_all, patches_all, heads_all * head_size)
    return jnp.concatenate([grad_query.reshape(flat_shape), grad_key.reshape(flat_shape), grad_value.reshape(flat_shape)], axis=-1)

def reference(qkv, keep, counts, grad_out, w_out):
    frame_ids = jnp.broadcast_to(jnp.arange(FRAMES, dtype=jnp.int32)[:, None], (FRAMES, CAP))

    def one_clip(carry, inputs):
        qkv_clip, keep_clip, count_clip, grad_clip = inputs
        live = jnp.arange(CAP, dtype=jnp.int32)[None, :] < count_clip[:, None]
        masked_in = jnp.where(live[..., None], qkv_clip, jnp.zeros((), jnp.bfloat16))
        grid = jnp.zeros((FRAMES, PATCHES, 3 * D), jnp.bfloat16).at[frame_ids, keep_clip].set(masked_in)
        kept = jnp.zeros((FRAMES, PATCHES), jnp.float32).at[frame_ids, keep_clip].set(live.astype(jnp.float32))
        att_grid, saved = attention_forward(grid, kept)
        att = jnp.take_along_axis(att_grid, keep_clip[..., None], axis=1)
        att = jnp.where(live[..., None], att, jnp.zeros((), jnp.bfloat16))
        att_flat = att.reshape(FRAMES * CAP, D)
        grad_flat = grad_clip.reshape(FRAMES * CAP, D)
        mixed = jnp.dot(att_flat, w_out, preferred_element_type=jnp.float32).astype(jnp.bfloat16)
        grad_att = jnp.dot(grad_flat, jnp.transpose(w_out), preferred_element_type=jnp.float32).astype(jnp.bfloat16)
        grad_att = jnp.where(live[..., None], grad_att.reshape(FRAMES, CAP, D), jnp.zeros((), jnp.bfloat16))
        weight_term = jnp.dot(jnp.transpose(att_flat), grad_flat, preferred_element_type=jnp.float32)
        grad_grid = jnp.zeros((FRAMES, PATCHES, D), jnp.bfloat16).at[frame_ids, keep_clip].set(grad_att)
        grad_qkv_grid = attention_backward(saved, grad_grid)
        grad_qkv = jnp.take_along_axis(grad_qkv_grid, keep_clip[..., None], axis=1)
        grad_qkv = jnp.where(live[..., None], grad_qkv, jnp.zeros((), jnp.bfloat16))
        return (carry + weight_term, (mixed.reshape(FRAMES, CAP, D), grad_qkv))
    weight_sum, outputs = lax.scan(one_clip, jnp.zeros((D, D), jnp.float32), (qkv, keep, counts, grad_out))
    mixed, grad_qkv = outputs
    return (mixed, grad_qkv, weight_sum * (1.0 / CLIPS))
```

```python
import functools
import math

import jax
import jax.numpy as jnp
from jax import lax
from jax.experimental import pallas as pl
from jax.experimental.pallas import tpu as pltpu
from jax.sharding import Mesh
from jax.sharding import PartitionSpec as P

HEADS = 16
PATCHES = 256
FRAMES = 8
CAP = 192
D = 1408
WIDE = D // FRAMES
HEAD = D // HEADS
SUB = 44
SUBP = 48
PACK = 640
GROUP = 16
BLOCK = GROUP * FRAMES
BIG = 1e30
VMEM = pltpu.VMEM
bf16 = jnp.bfloat16
f32 = jnp.float32


STEPS = [(0, 0), (0, 1), (3, 0), (3, 1), (1, 0), (1, 1), (2, 0), (2, 1)]
ALL = ("z", "y", "x", "core")
FRAME = ("x", "core")
WHERE, ORIGIN, Z_FLIP, Y_FLIP = 0, 8, 16, 24


def dot(a, b):
    return jnp.dot(a, b, preferred_element_type=f32)


def dot_t(a, b):
    return lax.dot_general(a, b, (((1,), (1,)), ((), ())), preferred_element_type=f32)


def t_dot(a, b):
    return lax.dot_general(a, b, (((0,), (0,)), ((), ())), preferred_element_type=f32)


def iota(shape, dim):
    return lax.broadcasted_iota(jnp.int32, shape, dim)


def call(kernel, out_shape, n_in, flops=0, scratch=(), smem=()):
    def spec(shape):
        return pl.BlockSpec(shape, lambda i: (0,) * len(shape), pipeline_mode=pl.Buffered(1))

    def run(*args):
        specs = [
            pl.BlockSpec(memory_space=pltpu.SMEM) if i in smem else spec(a.shape)
            for i, a in enumerate(args)
        ]
        return pl.pallas_call(
            kernel,
            grid=(1,),
            out_shape=out_shape,
            in_specs=specs,
            out_specs=jax.tree.map(lambda s: spec(s.shape), out_shape),
            scratch_shapes=list(scratch),
            compiler_params=pltpu.CompilerParams(vmem_limit_bytes=60 * 1024 * 1024),
            cost_estimate=pl.CostEstimate(flops=flops, bytes_accessed=0, transcendentals=0),
        )(*args)

    return run


def pack_kernel(counts_ref, qkv_ref, keep_ref, out_ref):
    keep = keep_ref[0, 0:1, :]
    slot = iota((CAP, CAP), 1)
    diag = iota((CAP, CAP), 0) == slot
    held = jnp.where(slot < counts_ref[0, 0], keep.astype(f32), -1.0)
    column = jnp.sum(jnp.where(diag, held, 0.0), axis=1, keepdims=True)
    tail = jnp.broadcast_to(column, (CAP, PACK - 3 * WIDE)).astype(bf16)
    for f in range(FRAMES):
        parts = [
            qkv_ref[0, 0, :, part * D + WIDE * f : part * D + WIDE * (f + 1)] for part in range(3)
        ]
        out_ref[f] = jnp.concatenate(parts + [tail], axis=1)


def rows_from(keep_column):
    diag = iota((CAP, CAP), 0) == iota((CAP, CAP), 1)
    return jnp.sum(jnp.where(diag, keep_column, 0.0), axis=0, keepdims=True)


def forward_kernel(
    recv_ref, att_ref, hot_ref, hot_t_ref, qg, kg, vg, probs_ref, ag
):
    scaling = 1.0 / math.sqrt(HEAD)
    lane = iota((PATCHES, PATCHES), 1)
    patch = lax.rem(iota((PATCHES, PATCHES), 0), GROUP)
    extra = lane >= WIDE
    q_extra = jnp.where((lane == WIDE) | (lane == WIDE + 1 + patch), 1.0, 0.0)
    pick = (lane > WIDE) & (lane <= WIDE + GROUP)
    k_extra = jnp.where(pick & (lane != WIDE + 1 + patch), -BIG, 0.0)
    zeros = jnp.zeros((CAP, PATCHES - WIDE), bf16)
    ones = jnp.ones((CAP, PATCHES - WIDE), bf16)
    for t in range(FRAMES):
        recv = recv_ref.at[t]
        column = recv[:, 3 * WIDE : 3 * WIDE + 1].astype(f32)
        row = rows_from(column)
        hot = jnp.where(column == iota((CAP, PATCHES), 1).astype(f32), 1.0, 0.0)
        hot_ref[t] = hot.astype(bf16)
        hot_t = jnp.where(row == iota((PATCHES, CAP), 0).astype(f32), 1.0, 0.0).astype(bf16)
        hot_t_ref[t] = jnp.concatenate([hot_t, jnp.zeros((PATCHES, PATCHES - CAP), bf16)], axis=1)
        q = recv[:, :WIDE]
        k = recv[:, WIDE : 2 * WIDE]
        v = recv[:, 2 * WIDE : 3 * WIDE]
        placed = dot(hot_t, jnp.concatenate([q, zeros, k, ones, v], axis=1))
        qg[t] = (placed[:, :PATCHES] + q_extra).astype(bf16)
        kk = placed[:, PATCHES : 2 * PATCHES]
        kk = jnp.where(extra, jnp.where(lane == WIDE, (kk - 1.0) * BIG, k_extra), kk)
        kg[t] = kk.astype(bf16)
        vg[t] = placed[:, 2 * PATCHES :].astype(bf16)

    wide_lane = iota((BLOCK, PATCHES), 1)
    first = (wide_lane < HEAD) | (wide_lane >= WIDE)
    second = wide_lane >= HEAD
    slim = iota((BLOCK, WIDE), 1) < HEAD
    for b in range(PATCHES // GROUP):
        rows = slice(b * GROUP, (b + 1) * GROUP)
        q = jnp.concatenate([qg[t, rows, :] for t in range(FRAMES)], axis=0)
        k = jnp.concatenate([kg[t, rows, :] for t in range(FRAMES)], axis=0)
        v = jnp.concatenate([vg[t, rows, :] for t in range(FRAMES)], axis=0)
        zero = jnp.zeros_like(q)
        q2 = jnp.concatenate([jnp.where(first, q, zero), jnp.where(second, q, zero)], axis=0)
        scores = dot_t(k, q2) * scaling
        expo = jnp.exp(scores - jnp.max(scores, axis=0, keepdims=True))
        probs = expo * (1.0 / jnp.sum(expo, axis=0, keepdims=True))
        probs_ref[b] = probs
        out = t_dot(probs.astype(bf16), v)
        att = jnp.where(slim, out[:BLOCK], out[BLOCK:]).astype(bf16)
        for t in range(FRAMES):
            ag[t, rows, :] = att[t * GROUP : (t + 1) * GROUP]
    tail = jnp.zeros((CAP, PATCHES - WIDE), bf16)
    for t in range(FRAMES):
        slots = dot(hot_ref[t], ag[t]).astype(bf16)
        att_ref[t] = jnp.concatenate([slots, tail], axis=1)


def backward_kernel(
    table_ref, grad_att_ref, att_ref, hot_ref, hot_t_ref, qg, kg, vg, probs_ref, *refs
):
    grad_ref, gg, dq, dk, dv = refs
    scaling = 1.0 / math.sqrt(HEAD)
    for i in range(FRAMES):
        t = table_ref[0, WHERE + i]
        gg[t] = dot(hot_t_ref[t][:, :CAP], grad_att_ref[i]).astype(bf16)
    slim = iota((BLOCK, WIDE), 1) < HEAD

    def two(x):
        zero = jnp.zeros_like(x)
        return jnp.concatenate([jnp.where(slim, x, zero), jnp.where(slim, zero, x)], axis=0)

    for b in range(PATCHES // GROUP):
        rows = slice(b * GROUP, (b + 1) * GROUP)
        q = jnp.concatenate([qg[t, rows, :WIDE] for t in range(FRAMES)], axis=0)
        k = jnp.concatenate([kg[t, rows, :WIDE] for t in range(FRAMES)], axis=0)
        v = jnp.concatenate([vg[t, rows, :] for t in range(FRAMES)], axis=0)
        g2 = two(jnp.concatenate([gg[t, rows, :] for t in range(FRAMES)], axis=0))
        probs = probs_ref[b]
        grad_probs = dot_t(v, g2)
        grad_v = dot(probs.astype(bf16), g2).astype(bf16)
        inner = jnp.sum(probs * grad_probs, axis=0, keepdims=True)
        grad_scores = (probs * (grad_probs - inner)).astype(bf16)
        out = t_dot(grad_scores, k)
        grad_q = (jnp.where(slim, out[:BLOCK], out[BLOCK:]) * scaling).astype(bf16)
        grad_k = (dot(grad_scores, two(q)) * scaling).astype(bf16)
        for t in range(FRAMES):
            own = slice(t * GROUP, (t + 1) * GROUP)
            dq[t, rows, :] = grad_q[own]
            dk[t, rows, :] = grad_k[own]
            dv[t, rows, :] = grad_v[own]
    for t in range(FRAMES):
        parts = [dot(hot_ref[t], x[t]).astype(bf16) for x in (dq, dk, dv)]
        grad_ref[t] = jnp.concatenate(parts + [att_ref[t, :, :WIDE]], axis=1)


def grad_att_kernel(w_ref, *refs):
    for i in range(FRAMES):
        refs[FRAMES][i] = dot_t(refs[i][...], w_ref[...]).astype(bf16)


def weight_kernel(table_ref, att_ref, *refs):
    keep_ref, send_ref, scr = refs[FRAMES:]
    total = None
    for i in range(FRAMES):
        term = t_dot(att_ref[table_ref[0, WHERE + i]][:, :WIDE], refs[i][...])
        total = term if total is None else total + term
    down = jnp.zeros((SUBP - SUB, D), f32)
    for s in range(4):
        scr[s] = jnp.concatenate([total[SUB * s : SUB * (s + 1)], down], axis=0)
    for r in range(2):
        keep_ref[r] = scr[table_ref[0, Y_FLIP + r]]
        send_ref[r] = scr[table_ref[0, Y_FLIP + 2 + r]].astype(bf16)


def halve_kernel(own_ref, in_ref, keep_ref, send_ref):
    half = own_ref.shape[0] // 2
    keep_ref[...] = own_ref[:half] + in_ref[:half].astype(f32)
    send_ref[...] = (own_ref[half:] + in_ref[half:].astype(f32)).astype(bf16)


def planes_kernel(table_ref, own_ref, in_ref, keep_ref, send_ref, scr):
    total = own_ref[0] + in_ref[0].astype(f32)
    for f in range(FRAMES):
        scr[f] = total[:, WIDE * f : WIDE * (f + 1)]
    for r in range(4):
        keep_ref[r] = scr[table_ref[0, Z_FLIP + r]]
        send_ref[r] = scr[table_ref[0, Z_FLIP + 4 + r]].astype(bf16)


def last_kernel(own_ref, in_ref, out_ref):
    out_ref[...] = ((own_ref[0] + in_ref[0].astype(f32)) * (1.0 / 32))[:SUB]


def columns_kernel(table_ref, *refs):
    out_ref, scr = refs[4:]
    at = 0
    for ref in refs[:4]:
        for i in range(ref.shape[0]):
            scr[table_ref[0, Z_FLIP + at]] = ref[i]
            at = at + 1
    out_ref[0] = jnp.concatenate([scr[f] for f in range(FRAMES)], axis=1)


def features_kernel(table_ref, one_ref, two_ref, four_ref, out_ref, scr):
    subs = [one_ref[0], two_ref[0], four_ref[0], four_ref[1]]
    for r in range(4):
        scr[table_ref[0, Y_FLIP + r]] = subs[r]
    out_ref[...] = jnp.concatenate([scr[s][:SUB] for s in range(4)], axis=0)


def final_kernel(table_ref, in_ref, *refs):
    mixed_ref, grad_ref = refs[FRAMES:]
    total = None
    for i in range(FRAMES):
        att = in_ref[table_ref[0, ORIGIN + i], :, 3 * WIDE :]
        term = dot(att, refs[i][...])
        total = term if total is None else total + term
    mixed_ref[0, 0] = total.astype(bf16)
    for part in range(3):
        pieces = [in_ref[f, :, part * WIDE : (part + 1) * WIDE] for f in range(FRAMES)]
        grad_ref[0, 0, :, part * D : (part + 1) * D] = jnp.concatenate(pieces, axis=1)


def shift(x, axis, count, k):
    return lax.ppermute(x, axis, [(i, (i + k) % count) for i in range(count)])


def device(z, y, f):
    return (z * 4 + y) * 8 + f


EVERY = [(z, y, f) for z in range(8) for y in range(4) for f in range(8)]


def flip(x, axis, count, mask):
    return lax.ppermute(x, axis, [(i, i ^ mask) for i in range(count)])


def turn(x):
    return lax.ppermute(x, ALL, [(device(z, y, f), device(f, y, z)) for z, y, f in EVERY])


def shards(qkv, keep, counts, grad_out, w_out):
    x_here = lax.axis_index("x").astype(jnp.int32)
    y_here = lax.axis_index("y").astype(jnp.int32)
    z_here = lax.axis_index("z").astype(jnp.int32)
    core = lax.axis_index("core").astype(jnp.int32)
    sds = jax.ShapeDtypeStruct
    swap = lambda a: shift(a, "core", 2, 1)
    table = [2 * lax.rem(x_here + dx, 4) + (core ^ dc) for dx, dc in STEPS]
    table += [2 * lax.rem(x_here + 4 - dx, 4) + (core ^ dc) for dx, dc in STEPS]
    table += [z_here ^ r for r in (0, 4, 2, 6, 1, 5, 3, 7)] + [y_here ^ r for r in (0, 2, 1, 3)]
    table = jnp.stack(table)[None]

    w_one = turn(jnp.pad(w_out, ((0, SUBP - SUB), (0, 0))))[None]
    packed = call(pack_kernel, sds((FRAMES, CAP, PACK), bf16), 3, smem=(0,))(counts, qkv, keep)
    recv = lax.all_to_all(packed, FRAME, 0, 0, tiled=True)
    w_two = flip(w_one, "z", 8, 4)
    w_four = flip(jnp.concatenate([w_one, w_two]), "z", 8, 2)
    w_eight = flip(jnp.concatenate([w_one, w_two, w_four]), "z", 8, 1)
    w_sub = call(
        columns_kernel,
        sds((1, SUBP, D), bf16),
        5,
        scratch=[VMEM((8, SUBP, WIDE), bf16)],
        smem=(0,),
    )(table, w_one, w_two, w_four, w_eight)
    w_next = flip(w_sub, "y", 4, 2)
    w_last = flip(jnp.concatenate([w_sub, w_next]), "y", 4, 1)
    g_chips = [grad_out[0, 0]]
    g_chips += [shift(g_chips[0], "x", 4, k) for k in (1, 3, 2)]
    g_all = [g for chip in g_chips for g in (chip, swap(chip))]

    grid = (FRAMES, PATCHES, PATCHES)
    slim = (FRAMES, PATCHES, WIDE)
    att, *saved = call(
        forward_kernel,
        (
            sds((FRAMES, CAP, PATCHES), bf16),
            sds((FRAMES, CAP, PATCHES), bf16),
            sds(grid, bf16),
            sds(grid, bf16),
            sds(grid, bf16),
            sds(slim, bf16),
            sds((PATCHES // GROUP, BLOCK, 2 * BLOCK), f32),
        ),
        1,
        scratch=[VMEM(slim, bf16)],
    )(recv)
    own, other = call(
        weight_kernel,
        (sds((2, SUBP, D), f32), sds((2, SUBP, D), bf16)),
        10,
        scratch=[VMEM((4, SUBP, D), f32)],
        smem=(0,),
    )(table, att, *g_all)
    other = flip(other, "y", 4, 1)
    w_last, own = lax.optimization_barrier((w_last, own))
    w_mine = call(
        features_kernel,
        sds((WIDE, D), bf16),
        4,
        scratch=[VMEM((4, SUBP, D), bf16)],
        smem=(0,),
    )(table, w_sub, w_next, w_last)
    grad_att = call(grad_att_kernel, sds((FRAMES, CAP, WIDE), bf16), 9)(w_mine, *g_all)
    other, _ = lax.optimization_barrier((other, grad_att))
    own, other = call(
        halve_kernel, (sds((1, SUBP, D), f32), sds((1, SUBP, D), bf16)), 2
    )(own, other)
    grad_att, own = lax.optimization_barrier((grad_att, own))
    grads = call(
        backward_kernel,
        sds((FRAMES, CAP, 4 * WIDE), bf16),
        9,
        scratch=[VMEM(slim, bf16)] * 4,
        smem=(0,),
    )(table, grad_att, att, *saved)
    w_chips = [w_mine] + [shift(w_mine, "x", 4, k) for k in (3, 1, 2)]
    grads, w_chips = lax.optimization_barrier((grads, w_chips))
    w_all = [w for chip in w_chips for w in (chip, swap(chip))]
    grad_back = lax.all_to_all(grads, FRAME, 0, 0, tiled=True)

    own, _ = lax.optimization_barrier((own, grads))
    own, other = call(
        planes_kernel,
        (sds((4, SUBP, WIDE), f32), sds((4, SUBP, WIDE), bf16)),
        3,
        scratch=[VMEM((8, SUBP, WIDE), f32)],
        smem=(0,),
    )(table, own, flip(other, "y", 4, 2))
    for mask, count in ((1, 2), (2, 1)):
        half = (count, SUBP, WIDE)
        own, other = call(halve_kernel, (sds(half, f32), sds(half, bf16)), 2)(
            own, flip(other, "z", 8, mask)
        )
    grad_weight = turn(call(last_kernel, sds((SUB, WIDE), f32), 2)(own, flip(other, "z", 8, 4)))

    mixed, grad_qkv = call(
        final_kernel,
        (sds((1, 1, CAP, D), bf16), sds((1, 1, CAP, 3 * D), bf16)),
        10,
        smem=(0,),
    )(table, grad_back, *w_all)
    return mixed, grad_qkv, grad_weight


def solution(mesh):
    fine = Mesh(mesh.devices.reshape(8, 4, 4, 2), ALL)
    dp = ("z", "y")
    return jax.shard_map(
        shards,
        mesh=fine,
        in_specs=(
            P(dp, FRAME, None, None),
            P(dp, FRAME, None),
            P(dp, FRAME),
            P(dp, FRAME, None, None),
            P(dp, FRAME),
        ),
        out_specs=(P(dp, FRAME, None, None), P(dp, FRAME, None, None), P(dp, FRAME)),
        check_vma=False,
    )
```

```python
import functools
import math

import jax
import jax.numpy as jnp
from jax import lax
from jax.experimental import pallas as pl
from jax.experimental.pallas import tpu as pltpu
from jax.sharding import Mesh
from jax.sharding import PartitionSpec as P

HEADS = 16
PATCHES = 256
FRAMES = 8
CAP = 192
D = 1408
WIDE = D // FRAMES
HEAD = D // HEADS
SUB = 44
PACK = 640
GROUP = 16
BLOCK = GROUP * FRAMES
BIG = 1e30
VMEM = pltpu.VMEM
bf16 = jnp.bfloat16
f32 = jnp.float32


STEPS = [(0, 0), (0, 1), (3, 0), (3, 1), (1, 0), (1, 1), (2, 0), (2, 1)]
ALL = ("z", "y", "x", "core")
FRAME = ("x", "core")
WHERE, ORIGIN, Z_FLIP, Y_FLIP, Y_NEXT = 0, 8, 16, 24, 28


def dot(a, b):
    return jnp.dot(a, b, preferred_element_type=f32)


def dot_t(a, b):
    return lax.dot_general(a, b, (((1,), (1,)), ((), ())), preferred_element_type=f32)


def t_dot(a, b):
    return lax.dot_general(a, b, (((0,), (0,)), ((), ())), preferred_element_type=f32)


def iota(shape, dim):
    return lax.broadcasted_iota(jnp.int32, shape, dim)


def call(kernel, out_shape, n_in, flops=0, scratch=(), smem=()):
    def spec(shape):
        return pl.BlockSpec(shape, lambda i: (0,) * len(shape), pipeline_mode=pl.Buffered(1))

    def run(*args):
        specs = [
            pl.BlockSpec(memory_space=pltpu.SMEM) if i in smem else spec(a.shape)
            for i, a in enumerate(args)
        ]
        return pl.pallas_call(
            kernel,
            grid=(1,),
            out_shape=out_shape,
            in_specs=specs,
            out_specs=jax.tree.map(lambda s: spec(s.shape), out_shape),
            scratch_shapes=list(scratch),
            compiler_params=pltpu.CompilerParams(vmem_limit_bytes=32 * 1024 * 1024),
            cost_estimate=pl.CostEstimate(flops=flops, bytes_accessed=0, transcendentals=0),
        )(*args)

    return run


def pack_kernel(counts_ref, qkv_ref, keep_ref, out_ref):
    keep = keep_ref[0, 0:1, :]
    slot = iota((CAP, CAP), 1)
    diag = iota((CAP, CAP), 0) == slot
    held = jnp.where(slot < counts_ref[0, 0], keep.astype(f32), -1.0)
    column = jnp.sum(jnp.where(diag, held, 0.0), axis=1, keepdims=True)
    tail = jnp.broadcast_to(column, (CAP, PACK - 3 * WIDE)).astype(bf16)
    for f in range(FRAMES):
        parts = [
            qkv_ref[0, 0, :, part * D + WIDE * f : part * D + WIDE * (f + 1)] for part in range(3)
        ]
        out_ref[f] = jnp.concatenate(parts + [tail], axis=1)


def rows_from(keep_column):
    diag = iota((CAP, CAP), 0) == iota((CAP, CAP), 1)
    return jnp.sum(jnp.where(diag, keep_column, 0.0), axis=0, keepdims=True)


def forward_kernel(
    recv_ref, att_ref, hot_ref, hot_t_ref, qg, kg, vg, probs_ref, ag
):
    scaling = 1.0 / math.sqrt(HEAD)
    lane = iota((PATCHES, PATCHES), 1)
    patch = lax.rem(iota((PATCHES, PATCHES), 0), GROUP)
    extra = lane >= WIDE
    q_extra = jnp.where((lane == WIDE) | (lane == WIDE + 1 + patch), 1.0, 0.0)
    pick = (lane > WIDE) & (lane <= WIDE + GROUP)
    k_extra = jnp.where(pick & (lane != WIDE + 1 + patch), -BIG, 0.0)
    zeros = jnp.zeros((CAP, PATCHES - WIDE), bf16)
    ones = jnp.ones((CAP, PATCHES - WIDE), bf16)
    for t in range(FRAMES):
        recv = recv_ref.at[t]
        column = recv[:, 3 * WIDE : 3 * WIDE + 1].astype(f32)
        row = rows_from(column)
        hot = jnp.where(column == iota((CAP, PATCHES), 1).astype(f32), 1.0, 0.0)
        hot_ref[t] = hot.astype(bf16)
        hot_t = jnp.where(row == iota((PATCHES, CAP), 0).astype(f32), 1.0, 0.0).astype(bf16)
        hot_t_ref[t] = jnp.concatenate([hot_t, jnp.zeros((PATCHES, PATCHES - CAP), bf16)], axis=1)
        q = recv[:, :WIDE]
        k = recv[:, WIDE : 2 * WIDE]
        v = recv[:, 2 * WIDE : 3 * WIDE]
        placed = dot(hot_t, jnp.concatenate([q, zeros, k, ones, v], axis=1))
        qg[t] = (placed[:, :PATCHES] + q_extra).astype(bf16)
        kk = placed[:, PATCHES : 2 * PATCHES]
        kk = jnp.where(extra, jnp.where(lane == WIDE, (kk - 1.0) * BIG, k_extra), kk)
        kg[t] = kk.astype(bf16)
        vg[t] = placed[:, 2 * PATCHES :].astype(bf16)

    wide_lane = iota((BLOCK, PATCHES), 1)
    first = (wide_lane < HEAD) | (wide_lane >= WIDE)
    second = wide_lane >= HEAD
    slim = iota((BLOCK, WIDE), 1) < HEAD
    for b in range(PATCHES // GROUP):
        rows = slice(b * GROUP, (b + 1) * GROUP)
        q = jnp.concatenate([qg[t, rows, :] for t in range(FRAMES)], axis=0)
        k = jnp.concatenate([kg[t, rows, :] for t in range(FRAMES)], axis=0)
        v = jnp.concatenate([vg[t, rows, :] for t in range(FRAMES)], axis=0)
        zero = jnp.zeros_like(q)
        q2 = jnp.concatenate([jnp.where(first, q, zero), jnp.where(second, q, zero)], axis=0)
        scores = dot_t(k, q2) * scaling
        expo = jnp.exp(scores - jnp.max(scores, axis=0, keepdims=True))
        probs = expo * (1.0 / jnp.sum(expo, axis=0, keepdims=True))
        probs_ref[b] = probs
        out = t_dot(probs.astype(bf16), v)
        att = jnp.where(slim, out[:BLOCK], out[BLOCK:]).astype(bf16)
        for t in range(FRAMES):
            ag[t, rows, :] = att[t * GROUP : (t + 1) * GROUP]
    tail = jnp.zeros((CAP, PATCHES - WIDE), bf16)
    for t in range(FRAMES):
        slots = dot(hot_ref[t], ag[t]).astype(bf16)
        att_ref[t] = jnp.concatenate([slots, tail], axis=1)


def backward_kernel(
    table_ref, grad_att_ref, att_ref, hot_ref, hot_t_ref, qg, kg, vg, probs_ref, *refs
):
    grad_ref, gg, dq, dk, dv = refs
    scaling = 1.0 / math.sqrt(HEAD)
    for i in range(FRAMES):
        t = table_ref[0, WHERE + i]
        gg[t] = dot(hot_t_ref[t][:, :CAP], grad_att_ref[i]).astype(bf16)
    slim = iota((BLOCK, WIDE), 1) < HEAD

    def two(x):
        zero = jnp.zeros_like(x)
        return jnp.concatenate([jnp.where(slim, x, zero), jnp.where(slim, zero, x)], axis=0)

    for b in range(PATCHES // GROUP):
        rows = slice(b * GROUP, (b + 1) * GROUP)
        q = jnp.concatenate([qg[t, rows, :WIDE] for t in range(FRAMES)], axis=0)
        k = jnp.concatenate([kg[t, rows, :WIDE] for t in range(FRAMES)], axis=0)
        v = jnp.concatenate([vg[t, rows, :] for t in range(FRAMES)], axis=0)
        g2 = two(jnp.concatenate([gg[t, rows, :] for t in range(FRAMES)], axis=0))
        probs = probs_ref[b]
        grad_probs = dot_t(v, g2)
        grad_v = dot(probs.astype(bf16), g2).astype(bf16)
        inner = jnp.sum(probs * grad_probs, axis=0, keepdims=True)
        grad_scores = (probs * (grad_probs - inner)).astype(bf16)
        out = t_dot(grad_scores, k)
        grad_q = (jnp.where(slim, out[:BLOCK], out[BLOCK:]) * scaling).astype(bf16)
        grad_k = (dot(grad_scores, two(q)) * scaling).astype(bf16)
        for t in range(FRAMES):
            own = slice(t * GROUP, (t + 1) * GROUP)
            dq[t, rows, :] = grad_q[own]
            dk[t, rows, :] = grad_k[own]
            dv[t, rows, :] = grad_v[own]
    for t in range(FRAMES):
        parts = [dot(hot_ref[t], x[t]).astype(bf16) for x in (dq, dk, dv)]
        grad_ref[t] = jnp.concatenate(parts + [att_ref[t, :, :WIDE]], axis=1)


def grad_att_kernel(w_ref, *refs):
    for i in range(FRAMES):
        refs[FRAMES][i] = dot_t(refs[i][...], w_ref[...]).astype(bf16)


def weight_kernel(table_ref, att_ref, *refs):
    out_refs, scr = refs[FRAMES : FRAMES + 4], refs[FRAMES + 4]
    total = None
    for i in range(FRAMES):
        term = t_dot(att_ref[table_ref[0, WHERE + i]][:, :WIDE], refs[i][...])
        total = term if total is None else total + term
    for s in range(4):
        scr[s] = total[SUB * s : SUB * (s + 1)]
    for k in range(4):
        out_refs[k][...] = scr[table_ref[0, Y_NEXT + k]].astype(out_refs[k].dtype)


def halve_kernel(own_ref, in_ref, keep_ref, send_ref):
    half = own_ref.shape[0] // 2
    keep_ref[...] = own_ref[:half] + in_ref[:half].astype(f32)
    send_ref[...] = (own_ref[half:] + in_ref[half:].astype(f32)).astype(send_ref.dtype)


def planes_kernel(table_ref, *refs):
    keep_ref, send_ref, scr = refs[4:]
    total = refs[0][...]
    for k in range(1, 4):
        total = total + refs[k][...].astype(f32)
    for f in range(FRAMES):
        scr[f] = total[:, WIDE * f : WIDE * (f + 1)]
    for r in range(4):
        keep_ref[r] = scr[table_ref[0, Z_FLIP + r]]
        send_ref[r] = scr[table_ref[0, Z_FLIP + 4 + r]].astype(bf16)


def last_kernel(one_ref, two_ref, out_ref):
    out_ref[...] = (one_ref[...] + two_ref[...]) * (1.0 / 32)


def columns_kernel(table_ref, *refs):
    out_ref, scr = refs[4:]
    at = 0
    for ref in refs[:4]:
        for i in range(ref.shape[0]):
            scr[table_ref[0, Z_FLIP + at]] = ref[i]
            at = at + 1
    out_ref[0] = jnp.concatenate([scr[f] for f in range(FRAMES)], axis=1)


def features_kernel(table_ref, one_ref, two_ref, four_ref, out_ref, scr):
    subs = [one_ref[0], two_ref[0], four_ref[0], four_ref[1]]
    for r in range(4):
        scr[table_ref[0, Y_FLIP + r]] = subs[r]
    out_ref[...] = jnp.concatenate([scr[s] for s in range(4)], axis=0)


def final_kernel(table_ref, in_ref, *refs):
    mixed_ref, grad_ref = refs[FRAMES:]
    total = None
    for i in range(FRAMES):
        att = in_ref[table_ref[0, ORIGIN + i], :, 3 * WIDE :]
        term = dot(att, refs[i][...])
        total = term if total is None else total + term
    mixed_ref[0, 0] = total.astype(bf16)
    for part in range(3):
        pieces = [in_ref[f, :, part * WIDE : (part + 1) * WIDE] for f in range(FRAMES)]
        grad_ref[0, 0, :, part * D : (part + 1) * D] = jnp.concatenate(pieces, axis=1)


def shift(x, axis, count, k):
    return lax.ppermute(x, axis, [(i, (i + k) % count) for i in range(count)])


def device(z, y, f):
    return (z * 4 + y) * 8 + f


EVERY = [(z, y, f) for z in range(8) for y in range(4) for f in range(8)]


def flip(x, axis, count, mask):
    return lax.ppermute(x, axis, [(i, i ^ mask) for i in range(count)])


def turn(x, mask=0):
    pairs = [(device(z, y, f), device(f, y, z ^ mask)) for z, y, f in EVERY]
    return lax.ppermute(x, ALL, pairs)


def turn_back(x, mask):
    pairs = [(device(z, y, f), device(f ^ mask, y, z)) for z, y, f in EVERY]
    return lax.ppermute(x, ALL, pairs)


def shards(qkv, keep, counts, grad_out, w_out):
    x_here = lax.axis_index("x").astype(jnp.int32)
    y_here = lax.axis_index("y").astype(jnp.int32)
    z_here = lax.axis_index("z").astype(jnp.int32)
    core = lax.axis_index("core").astype(jnp.int32)
    sds = jax.ShapeDtypeStruct
    swap = lambda a: shift(a, "core", 2, 1)
    table = [2 * lax.rem(x_here + dx, 4) + (core ^ dc) for dx, dc in STEPS]
    table += [2 * lax.rem(x_here + 4 - dx, 4) + (core ^ dc) for dx, dc in STEPS]
    table += [z_here ^ r for r in (0, 4, 2, 6, 1, 5, 3, 7)] + [y_here ^ r for r in (0, 2, 1, 3)]
    table += [lax.rem(y_here + k, 4) for k in range(4)]
    table = jnp.stack(table)[None]

    w_here = w_out[None]
    w_one, w_two = turn_back(w_here, 0), turn_back(w_here, 4)
    packed = call(pack_kernel, sds((FRAMES, CAP, PACK), bf16), 3, smem=(0,))(counts, qkv, keep)
    packed, g_own = lax.optimization_barrier((packed, grad_out[0, 0]))
    g_chips = [g_own]
    g_chips += [shift(g_chips[0], "x", 4, k) for k in (1, 3, 2)]
    packed, g_chips, w_one, w_two = lax.optimization_barrier((packed, g_chips, w_one, w_two))
    recv = lax.all_to_all(packed, FRAME, 0, 0, tiled=True)
    g_all = [g for chip in g_chips for g in (chip, swap(chip))]
    w_four = flip(jnp.concatenate([w_one, w_two]), "z", 8, 2)
    w_eight = flip(jnp.concatenate([w_one, w_two, w_four]), "z", 8, 1)
    w_sub = call(
        columns_kernel,
        sds((1, SUB, D), bf16),
        5,
        scratch=[VMEM((8, SUB, WIDE), bf16)],
        smem=(0,),
    )(table, w_one, w_two, w_four, w_eight)
    w_next = flip(w_sub, "y", 4, 2)
    w_last = flip(jnp.concatenate([w_sub, w_next]), "y", 4, 1)
    grid = (FRAMES, PATCHES, PATCHES)
    slim = (FRAMES, PATCHES, WIDE)
    att, *saved = call(
        forward_kernel,
        (
            sds((FRAMES, CAP, PATCHES), bf16),
            sds((FRAMES, CAP, PATCHES), bf16),
            sds(grid, bf16),
            sds(grid, bf16),
            sds(grid, bf16),
            sds(slim, bf16),
            sds((PATCHES // GROUP, BLOCK, 2 * BLOCK), f32),
        ),
        1,
        scratch=[VMEM(slim, bf16)],
    )(recv)
    w_last, att = lax.optimization_barrier((w_last, att))
    w_mine = call(
        features_kernel,
        sds((WIDE, D), bf16),
        4,
        scratch=[VMEM((4, SUB, D), bf16)],
        smem=(0,),
    )(table, w_sub, w_next, w_last)
    grad_att = call(grad_att_kernel, sds((FRAMES, CAP, WIDE), bf16), 9)(w_mine, *g_all)
    own, *other = call(
        weight_kernel,
        (sds((SUB, D), f32),) + (sds((SUB, D), bf16),) * 3,
        10,
        scratch=[VMEM((4, SUB, D), f32)],
        smem=(0,),
    )(table, att, *g_all)
    other = [shift(piece, "y", 4, k) for k, piece in zip((1, 2, 3), other)]
    grad_att, own = lax.optimization_barrier((grad_att, own))
    grads = call(
        backward_kernel,
        sds((FRAMES, CAP, 4 * WIDE), bf16),
        9,
        scratch=[VMEM(slim, bf16)] * 4,
        smem=(0,),
    )(table, grad_att, att, *saved)
    other, grads = lax.optimization_barrier((other, grads))
    own, other = call(
        planes_kernel,
        (sds((4, SUB, WIDE), f32), sds((4, SUB, WIDE), bf16)),
        5,
        scratch=[VMEM((8, SUB, WIDE), f32)],
        smem=(0,),
    )(table, own, *other)
    grads, other = lax.optimization_barrier((grads, other))
    w_mine, _ = lax.optimization_barrier((w_mine, recv))
    w_chips = [w_mine] + [shift(w_mine, "x", 4, k) for k in (3, 1, 2)]
    grads, w_chips = lax.optimization_barrier((grads, w_chips))
    w_all = [w for chip in w_chips for w in (chip, swap(chip))]
    grad_back = lax.all_to_all(grads, FRAME, 0, 0, tiled=True)

    other = flip(other, "z", 8, 1)
    for mask, count, kind in ((1, 2, bf16), (2, 1, f32)):
        half = (count, SUB, WIDE)
        own, other = call(halve_kernel, (sds(half, f32), sds(half, kind)), 2)(
            own, other if mask == 1 else flip(other, "z", 8, mask)
        )
    pieces = [turn(own[0]), turn(other[0], 4)]
    mixed, grad_qkv = call(
        final_kernel,
        (sds((1, 1, CAP, D), bf16), sds((1, 1, CAP, 3 * D), bf16)),
        10,
        smem=(0,),
    )(table, grad_back, *w_all)
    pieces, grad_qkv = lax.optimization_barrier((pieces, grad_qkv))
    grad_weight = call(last_kernel, sds((SUB, WIDE), f32), 2)(*pieces)
    return mixed, grad_qkv, grad_weight


def solution(mesh):
    fine = Mesh(mesh.devices.reshape(8, 4, 4, 2), ALL)
    dp = ("z", "y")
    return jax.shard_map(
        shards,
        mesh=fine,
        in_specs=(
            P(dp, FRAME, None, None),
            P(dp, FRAME, None),
            P(dp, FRAME),
            P(dp, FRAME, None, None),
            P(dp, FRAME),
        ),
        out_specs=(P(dp, FRAME, None, None), P(dp, FRAME, None, None), P(dp, FRAME)),
        check_vma=False,
    )
```

```python
import functools
import math

import jax
import jax.numpy as jnp
from jax import lax
from jax.experimental import pallas as pl
from jax.experimental.pallas import tpu as pltpu
from jax.sharding import Mesh
from jax.sharding import PartitionSpec as P

HEADS = 16
PATCHES = 256
FRAMES = 8
CAP = 192
D = 1408
WIDE = D // FRAMES
HEAD = D // HEADS
SUB = 44
LINE = 3 * WIDE
HALF = CAP // 2
PACK = 1152
GROUP = 16
BLOCK = GROUP * FRAMES
BIG = 1e30
VMEM = pltpu.VMEM
bf16 = jnp.bfloat16
f32 = jnp.float32


STEPS = [(0, 0), (0, 1), (3, 0), (3, 1), (1, 0), (1, 1), (2, 0), (2, 1)]
ALL = ("z", "y", "x", "core")
FRAME = ("x", "core")
WHERE, ORIGIN, Z_FLIP, Y_FLIP = 0, 8, 16, 24


def dot(a, b):
    return jnp.dot(a, b, preferred_element_type=f32)


def dot_t(a, b):
    return lax.dot_general(a, b, (((1,), (1,)), ((), ())), preferred_element_type=f32)


def t_dot(a, b):
    return lax.dot_general(a, b, (((0,), (0,)), ((), ())), preferred_element_type=f32)


def iota(shape, dim):
    return lax.broadcasted_iota(jnp.int32, shape, dim)


def call(kernel, out_shape, n_in, flops=0, scratch=(), smem=()):
    def spec(shape):
        return pl.BlockSpec(shape, lambda i: (0,) * len(shape), pipeline_mode=pl.Buffered(1))

    def run(*args):
        specs = [
            pl.BlockSpec(memory_space=pltpu.SMEM) if i in smem else spec(a.shape)
            for i, a in enumerate(args)
        ]
        return pl.pallas_call(
            kernel,
            grid=(1,),
            out_shape=out_shape,
            in_specs=specs,
            out_specs=jax.tree.map(lambda s: spec(s.shape), out_shape),
            scratch_shapes=list(scratch),
            compiler_params=pltpu.CompilerParams(vmem_limit_bytes=28 * 1024 * 1024),
            cost_estimate=pl.CostEstimate(flops=flops, bytes_accessed=0, transcendentals=0),
        )(*args)

    return run


def pack_kernel(counts_ref, qkv_ref, keep_ref, out_ref):
    keep = keep_ref[0, 0:1, :]
    slot = iota((CAP, CAP), 1)
    diag = iota((CAP, CAP), 0) == slot
    held = jnp.where(slot < counts_ref[0, 0], keep.astype(f32), -1.0)
    column = jnp.sum(jnp.where(diag, held, 0.0), axis=1, keepdims=True)
    column = column.astype(bf16)
    pad = jnp.zeros((HALF, PACK - 2 * LINE - 2), bf16)
    for f in range(FRAMES):
        parts = []
        for rows in (slice(0, HALF), slice(HALF, CAP)):
            for part in range(3):
                at = part * D + WIDE * f
                parts.append(qkv_ref[0, 0, rows, at : at + WIDE])
        parts += [column[:HALF], column[HALF:], pad]
        out_ref[f] = jnp.concatenate(parts, axis=1)


def rows_from(keep_column):
    diag = iota((CAP, CAP), 0) == iota((CAP, CAP), 1)
    return jnp.sum(jnp.where(diag, keep_column, 0.0), axis=0, keepdims=True)


def place_clip(recv_ref, hot_ref, hot_t_ref, qg, kg, vg):
    lane = iota((PATCHES, PATCHES), 1)
    patch = lax.rem(iota((PATCHES, PATCHES), 0), GROUP)
    extra = lane >= WIDE
    q_extra = jnp.where((lane == WIDE) | (lane == WIDE + 1 + patch), 1.0, 0.0)
    pick = (lane > WIDE) & (lane <= WIDE + GROUP)
    k_extra = jnp.where(pick & (lane != WIDE + 1 + patch), -BIG, 0.0)
    zeros = jnp.zeros((CAP, PATCHES - WIDE), bf16)
    ones = jnp.ones((CAP, PATCHES - WIDE), bf16)
    for t in range(FRAMES):
        packed = recv_ref[t]
        recv = jnp.concatenate([packed[:, :LINE], packed[:, LINE : 2 * LINE]], axis=0)
        column = [packed[:, 2 * LINE + i : 2 * LINE + i + 1] for i in range(2)]
        column = jnp.concatenate(column, axis=0).astype(f32)
        row = rows_from(column)
        hot = jnp.where(column == iota((CAP, PATCHES), 1).astype(f32), 1.0, 0.0)
        hot_ref[t] = hot.astype(bf16)
        hot_t = jnp.where(row == iota((PATCHES, CAP), 0).astype(f32), 1.0, 0.0).astype(bf16)
        hot_t_ref[t] = jnp.concatenate([hot_t, jnp.zeros((PATCHES, PATCHES - CAP), bf16)], axis=1)
        q = recv[:, :WIDE]
        k = recv[:, WIDE : 2 * WIDE]
        v = recv[:, 2 * WIDE : 3 * WIDE]
        placed = dot(hot_t, jnp.concatenate([q, zeros, k, ones, v], axis=1))
        qg[t] = (placed[:, :PATCHES] + q_extra).astype(bf16)
        kk = placed[:, PATCHES : 2 * PATCHES]
        kk = jnp.where(extra, jnp.where(lane == WIDE, (kk - 1.0) * BIG, k_extra), kk)
        kg[t] = kk.astype(bf16)
        vg[t] = placed[:, 2 * PATCHES :].astype(bf16)


def forward_kernel(recv_ref, att_ref, hot_ref, hot_t_ref, qg, kg, vg, ag):
    scaling = 1.0 / math.sqrt(HEAD)
    place_clip(recv_ref, hot_ref, hot_t_ref, qg, kg, vg)
    wide_lane = iota((BLOCK, PATCHES), 1)
    first = (wide_lane < HEAD) | (wide_lane >= WIDE)
    second = wide_lane >= HEAD
    slim = iota((BLOCK, WIDE), 1) < HEAD
    for b in range(PATCHES // GROUP):
        rows = slice(b * GROUP, (b + 1) * GROUP)
        q = jnp.concatenate([qg[t, rows, :] for t in range(FRAMES)], axis=0)
        k = jnp.concatenate([kg[t, rows, :] for t in range(FRAMES)], axis=0)
        v = jnp.concatenate([vg[t, rows, :] for t in range(FRAMES)], axis=0)
        zero = jnp.zeros_like(q)
        q2 = jnp.concatenate([jnp.where(first, q, zero), jnp.where(second, q, zero)], axis=0)
        scores = dot_t(k, q2) * scaling
        expo = jnp.exp(scores - jnp.max(scores, axis=0, keepdims=True))
        probs = expo * (1.0 / jnp.sum(expo, axis=0, keepdims=True))
        out = t_dot(probs.astype(bf16), v)
        att = jnp.where(slim, out[:BLOCK], out[BLOCK:]).astype(bf16)
        for t in range(FRAMES):
            ag[t, rows, :] = att[t * GROUP : (t + 1) * GROUP]
    tail = jnp.zeros((CAP, PATCHES - WIDE), bf16)
    for t in range(FRAMES):
        slots = dot(hot_ref[t], ag[t]).astype(bf16)
        att_ref[t] = jnp.concatenate([slots, tail], axis=1)


def backward_kernel(
    table_ref, grad_att_ref, att_ref, recv_ref, grad_ref, hot_ref, hot_t_ref, qg, kg, vg, gg
):
    scaling = 1.0 / math.sqrt(HEAD)
    place_clip(recv_ref, hot_ref, hot_t_ref, qg, kg, vg)
    for i in range(FRAMES):
        t = table_ref[0, WHERE + i]
        gg[t] = dot(hot_t_ref[t][:, :CAP], grad_att_ref[i]).astype(bf16)
    wide_lane = iota((BLOCK, PATCHES), 1)
    first = (wide_lane < HEAD) | (wide_lane >= WIDE)
    second = wide_lane >= HEAD
    slim = iota((BLOCK, WIDE), 1) < HEAD

    def two(x):
        zero = jnp.zeros_like(x)
        return jnp.concatenate([jnp.where(slim, x, zero), jnp.where(slim, zero, x)], axis=0)

    for b in range(PATCHES // GROUP):
        rows = slice(b * GROUP, (b + 1) * GROUP)
        q = jnp.concatenate([qg[t, rows, :] for t in range(FRAMES)], axis=0)
        k = jnp.concatenate([kg[t, rows, :] for t in range(FRAMES)], axis=0)
        v = jnp.concatenate([vg[t, rows, :] for t in range(FRAMES)], axis=0)
        g2 = two(jnp.concatenate([gg[t, rows, :] for t in range(FRAMES)], axis=0))
        zero = jnp.zeros_like(q)
        q2 = jnp.concatenate([jnp.where(first, q, zero), jnp.where(second, q, zero)], axis=0)
        scores = dot_t(k, q2) * scaling
        expo = jnp.exp(scores - jnp.max(scores, axis=0, keepdims=True))
        probs = expo * (1.0 / jnp.sum(expo, axis=0, keepdims=True))
        grad_probs = dot_t(v, g2)
        grad_v = dot(probs.astype(bf16), g2).astype(bf16)
        inner = jnp.sum(probs * grad_probs, axis=0, keepdims=True)
        grad_scores = (probs * (grad_probs - inner)).astype(bf16)
        out = t_dot(grad_scores, k[:, :WIDE])
        grad_q = (jnp.where(slim, out[:BLOCK], out[BLOCK:]) * scaling).astype(bf16)
        grad_k = (dot(grad_scores, q2[:, :WIDE]) * scaling).astype(bf16)
        for t in range(FRAMES):
            own = slice(t * GROUP, (t + 1) * GROUP)
            qg[t, rows, :WIDE] = grad_q[own]
            kg[t, rows, :WIDE] = grad_k[own]
            vg[t, rows, :] = grad_v[own]
    for t in range(FRAMES):
        parts = [dot(hot_ref[t], x[t, :, :WIDE]).astype(bf16) for x in (qg, kg, vg)]
        parts.append(att_ref[t, :, :WIDE])
        grad_ref[t] = jnp.concatenate(
            [x[:HALF] for x in parts] + [x[HALF:] for x in parts], axis=1
        )


def grad_att_kernel(w_ref, *refs):
    for i in range(FRAMES):
        refs[FRAMES][i] = dot_t(refs[i][...], w_ref[...]).astype(bf16)


def weight_kernel(table_ref, att_ref, *refs):
    out_ref = refs[FRAMES]
    total = None
    for i in range(FRAMES):
        term = t_dot(att_ref[table_ref[0, WHERE + i]][:, :WIDE], refs[i][...])
        total = term if total is None else total + term
    for s in range(4):
        out_ref[s] = total[SUB * s : SUB * (s + 1)].astype(bf16)


def halve_kernel(own_ref, in_ref, keep_ref, send_ref):
    half = own_ref.shape[0] // 2
    keep_ref[...] = own_ref[:half] + in_ref[:half].astype(f32)
    send_ref[...] = (own_ref[half:] + in_ref[half:].astype(f32)).astype(send_ref.dtype)


def planes_kernel(table_ref, in_ref, keep_ref, send_ref, scr):
    total = in_ref[0].astype(f32)
    for s in range(1, 4):
        total = total + in_ref[s].astype(f32)
    for f in range(FRAMES):
        scr[f] = total[:, WIDE * f : WIDE * (f + 1)]
    for r in range(4):
        keep_ref[r] = scr[table_ref[0, Z_FLIP + r]]
        send_ref[r] = scr[table_ref[0, Z_FLIP + 4 + r]].astype(bf16)


def last_kernel(one_ref, two_ref, out_ref):
    out_ref[...] = (one_ref[...] + two_ref[...]) * (1.0 / 32)


def columns_kernel(table_ref, *refs):
    out_ref, scr = refs[4:]
    at = 0
    for ref in refs[:4]:
        for i in range(ref.shape[0]):
            scr[table_ref[0, Z_FLIP + at]] = ref[i]
            at = at + 1
    out_ref[0] = jnp.concatenate([scr[f] for f in range(FRAMES)], axis=1)


def features_kernel(table_ref, one_ref, two_ref, four_ref, out_ref, scr):
    subs = [one_ref[0], two_ref[0], four_ref[0], four_ref[1]]
    for r in range(4):
        scr[table_ref[0, Y_FLIP + r]] = subs[r]
    out_ref[...] = jnp.concatenate([scr[s] for s in range(4)], axis=0)


def final_kernel(table_ref, in_ref, *refs):
    w_refs, mixed_ref, grad_ref = refs[:-2], refs[-2], refs[-1]
    for half in range(2):
        rows = slice(half * HALF, (half + 1) * HALF)
        base = half * 4 * WIDE
        total = None
        for i in range(FRAMES):
            att = in_ref[table_ref[0, ORIGIN + i], :, base + 3 * WIDE : base + 4 * WIDE]
            w = w_refs[0][i] if len(w_refs) == 1 else w_refs[i][...]
            term = dot(att, w)
            total = term if total is None else total + term
        mixed_ref[0, 0, rows, :] = total.astype(bf16)
        for part in range(3):
            at = base + part * WIDE
            pieces = [in_ref[f, :, at : at + WIDE] for f in range(FRAMES)]
            grad_ref[0, 0, rows, part * D : (part + 1) * D] = jnp.concatenate(pieces, axis=1)


def stack_kernel(*refs):
    for i in range(FRAMES):
        refs[FRAMES][i] = refs[i][...]


def shift(x, axis, count, k):
    return lax.ppermute(x, axis, [(i, (i + k) % count) for i in range(count)])


def device(z, y, f):
    return (z * 4 + y) * 8 + f


EVERY = [(z, y, f) for z in range(8) for y in range(4) for f in range(8)]


def flip(x, axis, count, mask):
    return lax.ppermute(x, axis, [(i, i ^ mask) for i in range(count)])


def turn(x, mask=0):
    pairs = [(device(z, y, f), device(f, y, z ^ mask)) for z, y, f in EVERY]
    return lax.ppermute(x, ALL, pairs)


def turn_back(x, mask):
    pairs = [(device(z, y, f), device(f ^ mask, y, z)) for z, y, f in EVERY]
    return lax.ppermute(x, ALL, pairs)


def shards(qkv, keep, counts, grad_out, w_out):
    x_here = lax.axis_index("x").astype(jnp.int32)
    y_here = lax.axis_index("y").astype(jnp.int32)
    z_here = lax.axis_index("z").astype(jnp.int32)
    core = lax.axis_index("core").astype(jnp.int32)
    sds = jax.ShapeDtypeStruct
    swap = lambda a: shift(a, "core", 2, 1)
    table = [2 * lax.rem(x_here + dx, 4) + (core ^ dc) for dx, dc in STEPS]
    table += [2 * lax.rem(x_here + 4 - dx, 4) + (core ^ dc) for dx, dc in STEPS]
    table += [z_here ^ r for r in (0, 4, 2, 6, 1, 5, 3, 7)] + [y_here ^ r for r in (0, 2, 1, 3)]
    table = jnp.stack(table)[None]

    w_here = w_out[None]
    w_one, w_two = turn_back(w_here, 0), turn_back(w_here, 4)
    packed = call(pack_kernel, sds((FRAMES, HALF, PACK), bf16), 3, smem=(0,))(counts, qkv, keep)
    packed, g_own = lax.optimization_barrier((packed, grad_out[0, 0]))
    g_chips = [g_own]
    g_chips += [shift(g_chips[0], "x", 4, k) for k in (1, 3, 2)]
    packed, g_chips, w_one, w_two = lax.optimization_barrier((packed, g_chips, w_one, w_two))
    recv = lax.all_to_all(packed, FRAME, 0, 0, tiled=True)
    g_all = [g for chip in g_chips for g in (chip, swap(chip))]
    w_four = flip(jnp.concatenate([w_one, w_two]), "z", 8, 2)
    w_eight = flip(jnp.concatenate([w_one, w_two, w_four]), "z", 8, 1)
    w_sub = call(
        columns_kernel,
        sds((1, SUB, D), bf16),
        5,
        scratch=[VMEM((8, SUB, WIDE), bf16)],
        smem=(0,),
    )(table, w_one, w_two, w_four, w_eight)
    w_next = flip(w_sub, "y", 4, 2)
    w_last = flip(jnp.concatenate([w_sub, w_next]), "y", 4, 1)
    grid = (FRAMES, PATCHES, PATCHES)
    slim = (FRAMES, PATCHES, WIDE)
    att = call(
        forward_kernel,
        sds((FRAMES, CAP, PATCHES), bf16),
        1,
        scratch=[
            VMEM((FRAMES, CAP, PATCHES), bf16),
            VMEM(grid, bf16),
            VMEM(grid, bf16),
            VMEM(grid, bf16),
            VMEM(slim, bf16),
            VMEM(slim, bf16),
        ],
    )(recv)
    w_last, att = lax.optimization_barrier((w_last, att))
    w_mine = call(
        features_kernel,
        sds((WIDE, D), bf16),
        4,
        scratch=[VMEM((4, SUB, D), bf16)],
        smem=(0,),
    )(table, w_sub, w_next, w_last)
    grad_att = call(grad_att_kernel, sds((FRAMES, CAP, WIDE), bf16), 9)(w_mine, *g_all)
    own = call(weight_kernel, sds((4, SUB, D), bf16), 10, smem=(0,))(table, att, *g_all)
    other = lax.all_to_all(own, "y", 0, 0, tiled=True)
    grad_att, own = lax.optimization_barrier((grad_att, own))
    grads = call(
        backward_kernel,
        sds((FRAMES, HALF, 8 * WIDE), bf16),
        4,
        scratch=[VMEM((FRAMES, CAP, PATCHES), bf16)] + [VMEM(grid, bf16)] * 3 + [VMEM(slim, bf16)] * 2,
        smem=(0,),
    )(table, grad_att, att, recv)
    other, grads = lax.optimization_barrier((other, grads))
    own, other = call(
        planes_kernel,
        (sds((4, SUB, WIDE), f32), sds((4, SUB, WIDE), bf16)),
        2,
        scratch=[VMEM((8, SUB, WIDE), f32)],
        smem=(0,),
    )(table, other)
    grads, other = lax.optimization_barrier((grads, other))
    w_mine, _ = lax.optimization_barrier((w_mine, recv))
    w_chips = [w_mine] + [shift(w_mine, "x", 4, k) for k in (3, 1, 2)]
    grads, w_chips = lax.optimization_barrier((grads, w_chips))
    w_all = [w for chip in w_chips for w in (chip, swap(chip))]
    grad_back = lax.all_to_all(grads, FRAME, 0, 0, tiled=True)

    other = flip(other, "z", 8, 1)
    w_stack = call(stack_kernel, sds((FRAMES, WIDE, D), bf16), 8)(*w_all)
    own, w_stack = lax.optimization_barrier((own, w_stack))
    for mask, count, kind in ((1, 2, bf16), (2, 1, f32)):
        half = (count, SUB, WIDE)
        own, other = call(halve_kernel, (sds(half, f32), sds(half, kind)), 2)(
            own, other if mask == 1 else flip(other, "z", 8, mask)
        )
    pieces = [turn(own[0]), turn(other[0], 4)]
    mixed, grad_qkv = call(
        final_kernel,
        (sds((1, 1, CAP, D), bf16), sds((1, 1, CAP, 3 * D), bf16)),
        3,
        smem=(0,),
    )(table, grad_back, w_stack)
    pieces, grad_qkv = lax.optimization_barrier((pieces, grad_qkv))
    grad_weight = call(last_kernel, sds((SUB, WIDE), f32), 2)(*pieces)
    return mixed, grad_qkv, grad_weight


def solution(mesh):
    fine = Mesh(mesh.devices.reshape(8, 4, 4, 2), ALL)
    dp = ("z", "y")
    return jax.shard_map(
        shards,
        mesh=fine,
        in_specs=(
            P(dp, FRAME, None, None),
            P(dp, FRAME, None),
            P(dp, FRAME),
            P(dp, FRAME, None, None),
            P(dp, FRAME),
        ),
        out_specs=(P(dp, FRAME, None, None), P(dp, FRAME, None, None), P(dp, FRAME)),
        check_vma=False,
    )
```

```python
import functools
import math

import jax
import jax.numpy as jnp
from jax import lax
from jax.experimental import pallas as pl
from jax.experimental.pallas import tpu as pltpu
from jax.sharding import Mesh
from jax.sharding import PartitionSpec as P

HEADS = 16
PATCHES = 256
FRAMES = 8
CAP = 192
D = 1408
WIDE = D // FRAMES
HEAD = D // HEADS
SUB = 44
LINE = 3 * WIDE
HALF = CAP // 2
PACK = 1152
GROUP = 16
BLOCK = GROUP * FRAMES
BIG = 1e30
VMEM = pltpu.VMEM
bf16 = jnp.bfloat16
f32 = jnp.float32


STEPS = [(0, 0), (0, 1), (3, 0), (3, 1), (1, 0), (1, 1), (2, 0), (2, 1)]
ALL = ("z", "y", "x", "core")
FRAME = ("x", "core")
WHERE, ORIGIN, Z_FLIP, Y_FLIP = 0, 8, 16, 24


def dot(a, b):
    return jnp.dot(a, b, preferred_element_type=f32)


def dot_t(a, b):
    return lax.dot_general(a, b, (((1,), (1,)), ((), ())), preferred_element_type=f32)


def t_dot(a, b):
    return lax.dot_general(a, b, (((0,), (0,)), ((), ())), preferred_element_type=f32)


def iota(shape, dim):
    return lax.broadcasted_iota(jnp.int32, shape, dim)


def call(kernel, out_shape, n_in, flops=0, scratch=(), smem=(), hbm=()):
    def spec(shape):
        return pl.BlockSpec(shape, lambda i: (0,) * len(shape), pipeline_mode=pl.Buffered(1))

    def run(*args):
        specs = [
            pl.BlockSpec(memory_space=pltpu.SMEM)
            if i in smem
            else pl.BlockSpec(memory_space=pltpu.HBM)
            if i in hbm
            else spec(a.shape)
            for i, a in enumerate(args)
        ]
        return pl.pallas_call(
            kernel,
            grid=(1,),
            out_shape=out_shape,
            in_specs=specs,
            out_specs=jax.tree.map(lambda s: spec(s.shape), out_shape),
            scratch_shapes=list(scratch),
            compiler_params=pltpu.CompilerParams(vmem_limit_bytes=28 * 1024 * 1024),
            cost_estimate=pl.CostEstimate(flops=flops, bytes_accessed=0, transcendentals=0),
        )(*args)

    return run


def pack_kernel(counts_ref, qkv_ref, keep_ref, out_ref):
    keep = keep_ref[0, 0:1, :]
    slot = iota((CAP, CAP), 1)
    diag = iota((CAP, CAP), 0) == slot
    held = jnp.where(slot < counts_ref[0, 0], keep.astype(f32), -1.0)
    column = jnp.sum(jnp.where(diag, held, 0.0), axis=1, keepdims=True)
    column = column.astype(bf16)
    pad = jnp.zeros((HALF, PACK - 2 * LINE - 2), bf16)
    for f in range(FRAMES):
        parts = []
        for rows in (slice(0, HALF), slice(HALF, CAP)):
            for part in range(3):
                at = part * D + WIDE * f
                parts.append(qkv_ref[0, 0, rows, at : at + WIDE])
        parts += [column[:HALF], column[HALF:], pad]
        out_ref[f] = jnp.concatenate(parts, axis=1)


def rows_from(keep_column):
    diag = iota((CAP, CAP), 0) == iota((CAP, CAP), 1)
    return jnp.sum(jnp.where(diag, keep_column, 0.0), axis=0, keepdims=True)


def place_clip(recv_ref, hot_ref, hot_t_ref, qg, kg, vg):
    lane = iota((PATCHES, PATCHES), 1)
    patch = lax.rem(iota((PATCHES, PATCHES), 0), GROUP)
    extra = lane >= WIDE
    q_extra = jnp.where((lane == WIDE) | (lane == WIDE + 1 + patch), 1.0, 0.0)
    pick = (lane > WIDE) & (lane <= WIDE + GROUP)
    k_extra = jnp.where(pick & (lane != WIDE + 1 + patch), -BIG, 0.0)
    zeros = jnp.zeros((CAP, PATCHES - WIDE), bf16)
    ones = jnp.ones((CAP, PATCHES - WIDE), bf16)
    for t in range(FRAMES):
        packed = recv_ref[t]
        recv = jnp.concatenate([packed[:, :LINE], packed[:, LINE : 2 * LINE]], axis=0)
        column = [packed[:, 2 * LINE + i : 2 * LINE + i + 1] for i in range(2)]
        column = jnp.concatenate(column, axis=0).astype(f32)
        row = rows_from(column)
        hot = jnp.where(column == iota((CAP, PATCHES), 1).astype(f32), 1.0, 0.0)
        hot_ref[t] = hot.astype(bf16)
        hot_t = jnp.where(row == iota((PATCHES, CAP), 0).astype(f32), 1.0, 0.0).astype(bf16)
        hot_t_ref[t] = jnp.concatenate([hot_t, jnp.zeros((PATCHES, PATCHES - CAP), bf16)], axis=1)
        q = recv[:, :WIDE]
        k = recv[:, WIDE : 2 * WIDE]
        v = recv[:, 2 * WIDE : 3 * WIDE]
        placed = dot(hot_t, jnp.concatenate([q, zeros, k, ones, v], axis=1))
        qg[t] = (placed[:, :PATCHES] + q_extra).astype(bf16)
        kk = placed[:, PATCHES : 2 * PATCHES]
        kk = jnp.where(extra, jnp.where(lane == WIDE, (kk - 1.0) * BIG, k_extra), kk)
        kg[t] = kk.astype(bf16)
        vg[t] = placed[:, 2 * PATCHES :].astype(bf16)


def forward_kernel(recv_ref, att_ref, hot_ref, hot_t_ref, qg, kg, vg, ag):
    scaling = 1.0 / math.sqrt(HEAD)
    place_clip(recv_ref, hot_ref, hot_t_ref, qg, kg, vg)
    wide_lane = iota((BLOCK, PATCHES), 1)
    first = (wide_lane < HEAD) | (wide_lane >= WIDE)
    second = wide_lane >= HEAD
    slim = iota((BLOCK, WIDE), 1) < HEAD
    for b in range(PATCHES // GROUP):
        rows = slice(b * GROUP, (b + 1) * GROUP)
        q = jnp.concatenate([qg[t, rows, :] for t in range(FRAMES)], axis=0)
        k = jnp.concatenate([kg[t, rows, :] for t in range(FRAMES)], axis=0)
        v = jnp.concatenate([vg[t, rows, :] for t in range(FRAMES)], axis=0)
        zero = jnp.zeros_like(q)
        q2 = jnp.concatenate([jnp.where(first, q, zero), jnp.where(second, q, zero)], axis=0)
        scores = dot_t(k, q2) * scaling
        expo = jnp.exp(scores - jnp.max(scores, axis=0, keepdims=True))
        probs = expo * (1.0 / jnp.sum(expo, axis=0, keepdims=True))
        out = t_dot(probs.astype(bf16), v)
        att = jnp.where(slim, out[:BLOCK], out[BLOCK:]).astype(bf16)
        for t in range(FRAMES):
            ag[t, rows, :] = att[t * GROUP : (t + 1) * GROUP]
    tail = jnp.zeros((CAP, PATCHES - WIDE), bf16)
    for t in range(FRAMES):
        slots = dot(hot_ref[t], ag[t]).astype(bf16)
        att_ref[t] = jnp.concatenate([slots, tail], axis=1)


def backward_kernel(
    table_ref, grad_att_ref, att_ref, recv_ref, grad_ref, hot_ref, hot_t_ref, qg, kg, vg, gg
):
    scaling = 1.0 / math.sqrt(HEAD)
    place_clip(recv_ref, hot_ref, hot_t_ref, qg, kg, vg)
    for i in range(FRAMES):
        t = table_ref[0, WHERE + i]
        gg[t] = dot(hot_t_ref[t][:, :CAP], grad_att_ref[i]).astype(bf16)
    wide_lane = iota((BLOCK, PATCHES), 1)
    first = (wide_lane < HEAD) | (wide_lane >= WIDE)
    second = wide_lane >= HEAD
    slim = iota((BLOCK, WIDE), 1) < HEAD

    def two(x):
        zero = jnp.zeros_like(x)
        return jnp.concatenate([jnp.where(slim, x, zero), jnp.where(slim, zero, x)], axis=0)

    for b in range(PATCHES // GROUP):
        rows = slice(b * GROUP, (b + 1) * GROUP)
        q = jnp.concatenate([qg[t, rows, :] for t in range(FRAMES)], axis=0)
        k = jnp.concatenate([kg[t, rows, :] for t in range(FRAMES)], axis=0)
        v = jnp.concatenate([vg[t, rows, :] for t in range(FRAMES)], axis=0)
        g2 = two(jnp.concatenate([gg[t, rows, :] for t in range(FRAMES)], axis=0))
        zero = jnp.zeros_like(q)
        q2 = jnp.concatenate([jnp.where(first, q, zero), jnp.where(second, q, zero)], axis=0)
        scores = dot_t(k, q2) * scaling
        expo = jnp.exp(scores - jnp.max(scores, axis=0, keepdims=True))
        probs = expo * (1.0 / jnp.sum(expo, axis=0, keepdims=True))
        grad_probs = dot_t(v, g2)
        grad_v = dot(probs.astype(bf16), g2).astype(bf16)
        inner = jnp.sum(probs * grad_probs, axis=0, keepdims=True)
        grad_scores = (probs * (grad_probs - inner)).astype(bf16)
        out = t_dot(grad_scores, k[:, :WIDE])
        grad_q = (jnp.where(slim, out[:BLOCK], out[BLOCK:]) * scaling).astype(bf16)
        grad_k = (dot(grad_scores, q2[:, :WIDE]) * scaling).astype(bf16)
        for t in range(FRAMES):
            own = slice(t * GROUP, (t + 1) * GROUP)
            qg[t, rows, :WIDE] = grad_q[own]
            kg[t, rows, :WIDE] = grad_k[own]
            vg[t, rows, :] = grad_v[own]
    for t in range(FRAMES):
        parts = [dot(hot_ref[t], x[t, :, :WIDE]).astype(bf16) for x in (qg, kg, vg)]
        parts.append(att_ref[t, :, :WIDE])
        grad_ref[t] = jnp.concatenate(
            [x[:HALF] for x in parts] + [x[HALF:] for x in parts], axis=1
        )


def grad_att_kernel(w_ref, *refs):
    for i in range(FRAMES):
        refs[FRAMES][i] = dot_t(refs[i][...], w_ref[...]).astype(bf16)


def weight_kernel(table_ref, att_ref, *refs):
    out_ref = refs[FRAMES]
    total = None
    for i in range(FRAMES):
        term = t_dot(att_ref[table_ref[0, WHERE + i]][:, :WIDE], refs[i][...])
        total = term if total is None else total + term
    for s in range(4):
        out_ref[s] = total[SUB * s : SUB * (s + 1)].astype(bf16)


def halve_kernel(own_ref, in_ref, keep_ref, send_ref):
    half = own_ref.shape[0] // 2
    keep_ref[...] = own_ref[:half] + in_ref[:half].astype(f32)
    send_ref[...] = (own_ref[half:] + in_ref[half:].astype(f32)).astype(send_ref.dtype)


def planes_kernel(table_ref, in_ref, keep_ref, send_ref, scr):
    total = in_ref[0].astype(f32)
    for s in range(1, 4):
        total = total + in_ref[s].astype(f32)
    for f in range(FRAMES):
        scr[f] = total[:, WIDE * f : WIDE * (f + 1)]
    for r in range(4):
        keep_ref[r] = scr[table_ref[0, Z_FLIP + r]]
        send_ref[r] = scr[table_ref[0, Z_FLIP + 4 + r]].astype(bf16)


def last_kernel(one_ref, two_ref, out_ref):
    out_ref[...] = (one_ref[...] + two_ref[...]) * (1.0 / 32)


def columns_kernel(table_ref, *refs):
    out_ref, scr = refs[4:]
    at = 0
    for ref in refs[:4]:
        for i in range(ref.shape[0]):
            scr[table_ref[0, Z_FLIP + at]] = ref[i]
            at = at + 1
    out_ref[0] = jnp.concatenate([scr[f] for f in range(FRAMES)], axis=1)


def features_kernel(table_ref, one_ref, two_ref, four_ref, out_ref, scr):
    subs = [one_ref[0], two_ref[0], four_ref[0], four_ref[1]]
    for r in range(4):
        scr[table_ref[0, Y_FLIP + r]] = subs[r]
    out_ref[...] = jnp.concatenate([scr[s] for s in range(4)], axis=0)


def final_kernel(table_ref, in_ref, *refs):
    mixed_ref, grad_ref, w_ref, sems = refs[FRAMES:]
    copies = [pltpu.make_async_copy(refs[i], w_ref.at[i], sems.at[i]) for i in range(FRAMES)]
    for copy in copies:
        copy.start()
    for half in range(2):
        rows = slice(half * HALF, (half + 1) * HALF)
        for part in range(3):
            at = half * 4 * WIDE + part * WIDE
            pieces = [in_ref[f, :, at : at + WIDE] for f in range(FRAMES)]
            grad_ref[0, 0, rows, part * D : (part + 1) * D] = jnp.concatenate(pieces, axis=1)
    for copy in copies:
        copy.wait()
    for half in range(2):
        rows = slice(half * HALF, (half + 1) * HALF)
        base = half * 4 * WIDE
        total = None
        for i in range(FRAMES):
            att = in_ref[table_ref[0, ORIGIN + i], :, base + 3 * WIDE : base + 4 * WIDE]
            term = dot(att, w_ref[i])
            total = term if total is None else total + term
        mixed_ref[0, 0, rows, :] = total.astype(bf16)


def shift(x, axis, count, k):
    return lax.ppermute(x, axis, [(i, (i + k) % count) for i in range(count)])


def device(z, y, f):
    return (z * 4 + y) * 8 + f


EVERY = [(z, y, f) for z in range(8) for y in range(4) for f in range(8)]


def flip(x, axis, count, mask):
    return lax.ppermute(x, axis, [(i, i ^ mask) for i in range(count)])


def turn(x, mask=0):
    pairs = [(device(z, y, f), device(f, y, z ^ mask)) for z, y, f in EVERY]
    return lax.ppermute(x, ALL, pairs)


def turn_back(x, mask):
    pairs = [(device(z, y, f), device(f ^ mask, y, z)) for z, y, f in EVERY]
    return lax.ppermute(x, ALL, pairs)


def shards(qkv, keep, counts, grad_out, w_out):
    x_here = lax.axis_index("x").astype(jnp.int32)
    y_here = lax.axis_index("y").astype(jnp.int32)
    z_here = lax.axis_index("z").astype(jnp.int32)
    core = lax.axis_index("core").astype(jnp.int32)
    sds = jax.ShapeDtypeStruct
    swap = lambda a: shift(a, "core", 2, 1)
    table = [2 * lax.rem(x_here + dx, 4) + (core ^ dc) for dx, dc in STEPS]
    table += [2 * lax.rem(x_here + 4 - dx, 4) + (core ^ dc) for dx, dc in STEPS]
    table += [z_here ^ r for r in (0, 4, 2, 6, 1, 5, 3, 7)] + [y_here ^ r for r in (0, 2, 1, 3)]
    table = jnp.stack(table)[None]

    w_here = w_out[None]
    w_one, w_two = turn_back(w_here, 0), turn_back(w_here, 4)
    packed = call(pack_kernel, sds((FRAMES, HALF, PACK), bf16), 3, smem=(0,))(counts, qkv, keep)
    packed, g_own = lax.optimization_barrier((packed, grad_out[0, 0]))
    g_chips = [g_own]
    g_chips += [shift(g_chips[0], "x", 4, k) for k in (1, 3, 2)]
    packed, g_chips, w_one, w_two = lax.optimization_barrier((packed, g_chips, w_one, w_two))
    recv = lax.all_to_all(packed, FRAME, 0, 0, tiled=True)
    g_all = [g for chip in g_chips for g in (chip, swap(chip))]
    w_four = flip(jnp.concatenate([w_one, w_two]), "z", 8, 2)
    w_eight = flip(jnp.concatenate([w_one, w_two, w_four]), "z", 8, 1)
    w_sub = call(
        columns_kernel,
        sds((1, SUB, D), bf16),
        5,
        scratch=[VMEM((8, SUB, WIDE), bf16)],
        smem=(0,),
    )(table, w_one, w_two, w_four, w_eight)
    w_next = flip(w_sub, "y", 4, 2)
    w_last = flip(jnp.concatenate([w_sub, w_next]), "y", 4, 1)
    grid = (FRAMES, PATCHES, PATCHES)
    slim = (FRAMES, PATCHES, WIDE)
    att = call(
        forward_kernel,
        sds((FRAMES, CAP, PATCHES), bf16),
        1,
        scratch=[
            VMEM((FRAMES, CAP, PATCHES), bf16),
            VMEM(grid, bf16),
            VMEM(grid, bf16),
            VMEM(grid, bf16),
            VMEM(slim, bf16),
            VMEM(slim, bf16),
        ],
    )(recv)
    w_last, att = lax.optimization_barrier((w_last, att))
    w_mine = call(
        features_kernel,
        sds((WIDE, D), bf16),
        4,
        scratch=[VMEM((4, SUB, D), bf16)],
        smem=(0,),
    )(table, w_sub, w_next, w_last)
    grad_att = call(grad_att_kernel, sds((FRAMES, CAP, WIDE), bf16), 9)(w_mine, *g_all)
    own = call(weight_kernel, sds((4, SUB, D), bf16), 10, smem=(0,))(table, att, *g_all)
    other = lax.all_to_all(own, "y", 0, 0, tiled=True)
    grad_att, own = lax.optimization_barrier((grad_att, own))
    grads = call(
        backward_kernel,
        sds((FRAMES, HALF, 8 * WIDE), bf16),
        4,
        scratch=[VMEM((FRAMES, CAP, PATCHES), bf16)] + [VMEM(grid, bf16)] * 3 + [VMEM(slim, bf16)] * 2,
        smem=(0,),
    )(table, grad_att, att, recv)
    other, grads = lax.optimization_barrier((other, grads))
    own, other = call(
        planes_kernel,
        (sds((4, SUB, WIDE), f32), sds((4, SUB, WIDE), bf16)),
        2,
        scratch=[VMEM((8, SUB, WIDE), f32)],
        smem=(0,),
    )(table, other)
    grads, other = lax.optimization_barrier((grads, other))
    w_mine, _ = lax.optimization_barrier((w_mine, recv))
    w_chips = [w_mine] + [shift(w_mine, "x", 4, k) for k in (3, 1, 2)]
    grads, w_chips = lax.optimization_barrier((grads, w_chips))
    w_all = [w for chip in w_chips for w in (chip, swap(chip))]
    grad_back = lax.all_to_all(grads, FRAME, 0, 0, tiled=True)

    other = flip(other, "z", 8, 1)
    for mask, count, kind in ((1, 2, bf16), (2, 1, f32)):
        half = (count, SUB, WIDE)
        own, other = call(halve_kernel, (sds(half, f32), sds(half, kind)), 2)(
            own, other if mask == 1 else flip(other, "z", 8, mask)
        )
    pieces = [turn(own[0]), turn(other[0], 4)]
    mixed, grad_qkv = call(
        final_kernel,
        (sds((1, 1, CAP, D), bf16), sds((1, 1, CAP, 3 * D), bf16)),
        10,
        scratch=[VMEM((FRAMES, WIDE, D), bf16), pltpu.SemaphoreType.DMA((FRAMES,))],
        smem=(0,),
        hbm=range(2, 10),
    )(table, grad_back, *w_all)
    pieces, grad_qkv = lax.optimization_barrier((pieces, grad_qkv))
    grad_weight = call(last_kernel, sds((SUB, WIDE), f32), 2)(*pieces)
    return mixed, grad_qkv, grad_weight


def solution(mesh):
    fine = Mesh(mesh.devices.reshape(8, 4, 4, 2), ALL)
    dp = ("z", "y")
    return jax.shard_map(
        shards,
        mesh=fine,
        in_specs=(
            P(dp, FRAME, None, None),
            P(dp, FRAME, None),
            P(dp, FRAME),
            P(dp, FRAME, None, None),
            P(dp, FRAME),
        ),
        out_specs=(P(dp, FRAME, None, None), P(dp, FRAME, None, None), P(dp, FRAME)),
        check_vma=False,
    )
```
